128 devices in a mesh: row: 16 (over y, x_lo, core), col: 8 (over z, x_hi).
Axes of the slice: x: 4 (x_hi: 2, x_lo: 2; x = x_hi * 2 + x_lo), y: 4, z: 4, core: 2. Of those that a mesh axis runs over, the one named last changes fastest.
Arguments:
- band_blocks: bfloat16 [256, 5, 512, 512], P(('row', 'col')), as said below
- occupancy: int32 [256, 5], P(('row', 'col')), may hold values from 0 to 1, as said below
Outputs:
- next_iterate: bfloat16 [256, 5, 512, 512], P(('row', 'col'))
The draws below stay inside these ranges and needn't reach their ends.
Inputs may be any that keep to these rules, and one draw needn't show every extreme that they name: `band_blocks`: the matrix is symmetric: the block in block row i and block column j is the transpose of the block in block row j and block column i. `occupancy`: the pattern is symmetric and every diagonal block is occupied.
All inputs are finite; a program needn't handle non-finite values.
Results may differ from the reference program's by a relative error of at most 0.0038.
Values may be sent and summed in bfloat16 or wider, within the bound.
A program may use at most 128 MiB of HBM per device.

```python
import jax
import jax.numpy as jnp
from jax import lax

B = 512
W = 2
SLOTS = 5
NB = 256


def mirror_blocks(upper_part, half_width):
    diagonal = (upper_part[:, half_width] + jnp.swapaxes(upper_part[:, half_width], -1, -2)) * 0.7071
    blocks = []
    for position in range(2 * half_width + 1):
        if position > half_width:
            blocks.append(upper_part[:, position])
        elif position == half_width:
            blocks.append(diagonal)
        else:
            offset = half_width - position
            blocks.append(jnp.roll(jnp.swapaxes(upper_part[:, half_width + offset], -1, -2), offset, axis=0))
    return jnp.stack(blocks, axis=1)


def draw_band_blocks(key, part):
    key = jax.random.fold_in(key, 11)
    full_shape = (NB, SLOTS, B, B)
    upper_part = jax.random.normal(key, full_shape, jnp.float32)
    return mirror_blocks(upper_part, W).astype(jnp.bfloat16)


def draw_occupancy(key, part):
    key = jax.random.fold_in(key, 23)
    drawn = jax.random.randint(key, (NB, SLOTS), 0, 4)
    upper_part = (drawn < 3).astype(jnp.int32)
    columns = []
    for position in range(SLOTS):
        if position > W:
            columns.append(upper_part[:, position])
        elif position == W:
            columns.append(jnp.ones((NB,), jnp.int32))
        else:
            offset = W - position
            columns.append(jnp.roll(upper_part[:, W + offset], offset, axis=0))
    return jnp.stack(columns, axis=1)


def setup_inputs(seed: int = 0) -> dict:
    streams_of = jax.random.split(jax.random.key(seed), 3)
    band_blocks = draw_band_blocks(jax.random.fold_in(streams_of[2], 71), 0)
    occupancy = draw_occupancy(jax.random.fold_in(streams_of[2], 71), 0)
    return {"band_blocks": band_blocks, "occupancy": occupancy}


def banded_product(left_band, right_band, keep_float):
    slot_count = left_band.shape[1]
    half_width = (slot_count - 1) // 2
    row_total = left_band.shape[0]
    padded = jnp.concatenate([right_band[row_total - half_width:], right_band, right_band[:half_width]], axis=0)

    def one_row(row_index):
        nearby = lax.dynamic_slice_in_dim(padded, row_index, slot_count, 0)
        own_row = lax.dynamic_index_in_dim(left_band, row_index, 0, keepdims=False)
        keep_row = lax.dynamic_index_in_dim(keep_float, row_index, 0, keepdims=False)
        results = []
        for out_slot in range(slot_count):
            summed = jnp.zeros(own_row.shape[1:], jnp.float32)
            for left_slot in range(slot_count):
                right_slot = out_slot - left_slot + half_width
                if 0 <= right_slot < slot_count:
                    summed = summed + jnp.dot(own_row[left_slot], nearby[left_slot, right_slot], preferred_element_type=jnp.float32)
            results.append(summed * keep_row[out_slot])
        return jnp.stack(results)

    return lax.map(one_row, jnp.arange(row_total, dtype=jnp.int32))


def reference(band_blocks, occupancy):
    keep_float = occupancy.astype(jnp.float32)
    masked = band_blocks * occupancy.astype(jnp.bfloat16)[:, :, None, None]
    square = banded_product(masked, masked, keep_float).astype(jnp.bfloat16)
    cubic = banded_product(square, masked, keep_float)
    factor = 0.5 / (band_blocks.shape[1] * band_blocks.shape[3])
    return (1.5 * masked.astype(jnp.float32) - factor * cubic).astype(jnp.bfloat16)
```

```python
import jax
import jax.numpy as jnp
from jax import lax
from jax.experimental import pallas as pl
from jax.experimental.pallas import tpu as pltpu
from jax.sharding import PartitionSpec as P

F32, BF16 = jnp.float32, jnp.bfloat16
MESH = pl.DeviceIdType.MESH
B = 512
H = B // 2
OWN = 2
SLOTS = 5
SPAN = 6
MIB = 2**20


def chain(step):
    rows, cols = lax.axis_size("row"), lax.axis_size("col")
    place = lax.axis_index("row") * cols + lax.axis_index("col")
    other = lax.rem(place + (step + rows * cols), rows * cols)
    return {"row": lax.div(other, cols), "col": lax.rem(other, cols)}


def at(ref, row, col, height=1, width=1):
    return ref.at[row * B : (row + height) * B, col * B : (col + width) * B]


def product(left, right):
    return jnp.dot(left, right, preferred_element_type=F32)


def triangles():
    row = lax.broadcasted_iota(jnp.int32, (H, H), 0)
    col = lax.broadcasted_iota(jnp.int32, (H, H), 1)
    return row, col


def pack(first, second):
    row, col = triangles()
    first, second = first.astype(F32), second.astype(F32)
    tile = jnp.where(row <= col, first, second).astype(BF16)
    diagonal = jnp.sum(jnp.where(row == col, second, 0.0), axis=0, keepdims=True)
    return tile, diagonal


def unpack(tile, diagonal):
    row, col = triangles()
    tile = tile.astype(F32)
    turned = tile.T
    first = jnp.where(row <= col, tile, turned)
    second = jnp.where(row > col, tile, jnp.where(row < col, turned, diagonal))
    return first.astype(BF16), second.astype(BF16)


def halves(body):
    def step(n, carry):
        body(pl.multiple_of(n * H, H))
        return carry

    lax.fori_loop(0, 2, step, 0)


def kernel(
    band, occupancy, out,
    x, s, total, partial, done, send0, send1, low0, low1, high0, high1,
    load_sem, store_sem, send_sem, recv_sem,
):
    after, before = chain(1), chain(-1)
    barrier = pltpu.get_barrier_semaphore()
    for neighbour in (after, before):
        pl.semaphore_signal(barrier, inc=1, device_id=neighbour, device_id_type=MESH)

    def keep(row, col):
        return occupancy[row - OWN, col - (row - OWN)].astype(F32)

    own = [(row, col) for row in (2, 3) for col in range(row - 2, row + 3)]
    first = [(2, 3), (2, 2), (3, 3)]
    order = first + [pair for pair in own if pair not in first]
    loads = {}
    for n, (row, col) in enumerate(order):
        loads[row, col] = pltpu.make_async_copy(
            band.at[row - 2, col - (row - 2)], at(x, row, col), load_sem.at[n]
        )
        loads[row, col].start()

    def loaded(row, col):
        loads[row, col].wait()
        block = at(x, row, col)
        block[...] = (block[...].astype(F32) * keep(row, col)).astype(BF16)

    def send(piece, source, to_after, to_before):
        copies = []
        for side, (target, landing) in enumerate(((after, to_after), (before, to_before))):
            copy = pltpu.make_async_remote_copy(
                src_ref=source,
                dst_ref=landing,
                send_sem=send_sem.at[side, piece],
                recv_sem=recv_sem.at[side, piece],
                device_id=target,
                device_id_type=MESH,
            )
            copy.start()
            copies.append(copy)
        return copies

    loaded(2, 3)
    pl.semaphore_wait(barrier, 2)
    sent_a = send(0, at(x, 2, 3), at(x, 0, 1), at(x, 4, 5))
    loaded(2, 2)
    loaded(3, 3)
    a, b = at(x, 2, 2), at(x, 3, 3)
    tile, diagonal0 = pack(a[:H, :H], b[:H, :H])
    send0[:H, :H] = tile
    tile, diagonal1 = pack(a[H:, H:], b[H:, H:])
    send1[...] = tile
    send0[:H, H : 2 * H] = a[:H, H:]
    send0[:H, 2 * H :] = b[:H, H:]
    diagonals = jnp.concatenate([diagonal0, diagonal1, jnp.zeros((1, H), F32)], axis=1)
    send0[H:, :] = jnp.broadcast_to(diagonals, (16, 3 * H)).astype(BF16)
    sent_0 = send(1, send0, low0, high0)
    sent_1 = send(2, send1, low1, high1)

    for pair in order[3:]:
        loaded(*pair)
    for row, col in ((2, 0), (2, 1), (3, 1), (2, 4), (3, 4), (3, 5)):
        at(x, col, row)[...] = at(x, row, col)[...].T

    def square(row, col, low, high, scale):
        left = x[row * B : (row + 1) * B, low * B : high * B]

        def body(c):
            right = x[low * B : high * B, pl.ds(col * B + c, H)]
            value = product(left, right) * scale
            s[(row - 2) * B : (row - 1) * B, pl.ds(col * B + c, H)] = value.astype(BF16)

        halves(body)

    square(2, 2, 0, 5, keep(2, 2))
    square(3, 3, 1, 6, keep(3, 3))
    square(2, 3, 1, 5, keep(2, 3))
    at(s, 1, 2)[...] = at(s, 0, 3)[...].T

    def begin(row, col, low, high):
        left = s[(row - 2) * B : (row - 1) * B, low * B : high * B]

        def body(c):
            right = x[low * B : high * B, pl.ds(col * B + c, H)]
            total[(row - 2) * B : (row - 1) * B, pl.ds(col * B + c, H)] = product(left, right)

        halves(body)

    for row, col in own:
        begin(row, col, max(2, col - 2), min(4, col + 3))

    def part(n, row, col, low, high):
        left = x[row * B : (row + 1) * B, low * B : high * B]

        def body(c):
            right = x[low * B : high * B, pl.ds(col * B + c, H)]
            partial[:, pl.ds(n * B + c, H)] = product(left, right)

        halves(body)

    part(0, 2, 4, 2, 4)
    part(1, 3, 4, 2, 4)
    part(2, 3, 5, 3, 4)

    def unpack_a(corner):
        at(x, corner + 1, corner)[...] = at(x, corner, corner + 1)[...].T

    def unpack_0(corner, piece):
        upper, lower = unpack(piece[:H, :H], piece[H : H + 1, :H].astype(F32))
        for n, tile in enumerate((upper, lower)):
            base = (corner + n) * B
            x[base : base + H, base : base + H] = tile
            side = piece[:H, (n + 1) * H : (n + 2) * H]
            x[base : base + H, base + H : base + B] = side
            x[base + H : base + B, base : base + H] = side.T

    def unpack_1(corner, piece, first_piece):
        upper, lower = unpack(piece[...], first_piece[H : H + 1, H : 2 * H].astype(F32))
        for n, tile in enumerate((upper, lower)):
            base = (corner + n) * B
            x[base + H : base + B, base + H : base + B] = tile

    def finish(row, col):
        scale = keep(row, col) / (2.0 * SLOTS * B)
        block = 1.5 * at(x, row, col)[...].astype(F32) - scale * at(total, row - 2, col)[...]
        done[row - 2, col - (row - 2)] = block.astype(BF16)

    stores = []

    def store(row, col):
        copy = pltpu.make_async_copy(
            done.at[row - 2, col - (row - 2)], out.at[row - 2, col - (row - 2)], store_sem.at[row - 2, col - (row - 2)]
        )
        copy.start()
        stores.append(copy)

    sent_a[0].wait_recv()
    unpack_a(0)
    sent_0[0].wait_recv()
    unpack_0(0, low0)
    sent_1[0].wait_recv()
    unpack_1(0, low1, low0)
    square(2, 0, 0, 3, keep(2, 0))
    square(2, 1, 0, 4, keep(2, 1))
    square(3, 1, 1, 4, keep(3, 1))

    def add(row, col, low, high):
        left = s[(row - 2) * B : (row - 1) * B, low * B : high * B]

        def body(c):
            right = x[low * B : high * B, pl.ds(col * B + c, H)]
            total[(row - 2) * B : (row - 1) * B, pl.ds(col * B + c, H)] += product(left, right)

        halves(body)

    add(2, 0, 0, 2)
    add(2, 1, 0, 2)
    add(2, 2, 0, 2)
    add(2, 3, 1, 2)
    add(3, 1, 1, 2)
    add(3, 2, 1, 2)
    add(3, 3, 1, 2)
    for pair in ((2, 0), (2, 1), (3, 1)):
        finish(*pair)
        store(*pair)

    def square_high(c):
        scale = keep(2, 4)
        value = partial[:, c : c + H] + product(x[2 * B : 3 * B, 4 * B : 5 * B], x[4 * B : 5 * B, 4 * B + c : 4 * B + c + H])
        s[:B, 4 * B + c : 4 * B + c + H] = (value * scale).astype(BF16)
        for n in (0, 1):
            scale = keep(3, 4 + n)
            begin_col = (4 + n) * B + c
            value = partial[:, (n + 1) * B + c : (n + 1) * B + c + H]
            value += product(x[3 * B : 4 * B, 4 * B : 6 * B], x[4 * B : 6 * B, begin_col : begin_col + H])
            s[B:, begin_col : begin_col + H] = (value * scale).astype(BF16)

    def add_high(c, row, col):
        values = []
        blocks = [4] if row == 2 or col == 2 else [4, 5]
        for k in blocks:
            left = s[(row - 2) * B : (row - 1) * B, k * B + c : k * B + c + H]
            values.append(product(left, x[k * B + c : k * B + c + H, col * B : (col + 1) * B]))
        at(total, row - 2, col)[...] += sum(values[1:], values[0])

    touched = [(2, 2), (2, 3), (2, 4), (3, 2), (3, 3), (3, 4), (3, 5)]
    sent_a[1].wait_recv()
    unpack_a(4)
    sent_0[1].wait_recv()
    unpack_0(4, high0)
    square_high(0)
    for pair in touched:
        add_high(0, *pair)
    sent_1[1].wait_recv()
    unpack_1(4, high1, high0)
    square_high(H)
    for pair in touched:
        add_high(H, *pair)
        finish(*pair)
        store(*pair)
    for copies in (sent_a, sent_0, sent_1):
        for copy in copies:
            copy.wait_send()
    for copy in stores:
        copy.wait()


def on_device(band_blocks, occupancy):
    dma = pltpu.SemaphoreType.DMA
    return pl.pallas_call(
        kernel,
        out_shape=jax.ShapeDtypeStruct(band_blocks.shape, BF16),
        in_specs=[pl.BlockSpec(memory_space=pl.ANY), pl.BlockSpec(memory_space=pltpu.SMEM)],
        out_specs=pl.BlockSpec(memory_space=pl.ANY),
        scratch_shapes=[
            pltpu.VMEM((SPAN * B, SPAN * B), BF16),
            pltpu.VMEM((OWN * B, SPAN * B), BF16),
            pltpu.VMEM((OWN * B, SPAN * B), F32),
            pltpu.VMEM((B, 3 * B), F32),
            pltpu.VMEM((OWN, SLOTS, B, B), BF16),
            pltpu.VMEM((H + 16, 3 * H), BF16),
            pltpu.VMEM((H, H), BF16),
            pltpu.VMEM((H + 16, 3 * H), BF16),
            pltpu.VMEM((H, H), BF16),
            pltpu.VMEM((H + 16, 3 * H), BF16),
            pltpu.VMEM((H, H), BF16),
            dma((OWN * SLOTS,)),
            dma((OWN, SLOTS)),
            dma((2, 3)),
            dma((2, 3)),
        ],
        compiler_params=pltpu.CompilerParams(
            collective_id=0, has_side_effects=True, vmem_limit_bytes=60 * MIB
        ),
        name="step",
    )(band_blocks, occupancy)


def solution(mesh):
    return jax.shard_map(
        on_device,
        mesh=mesh,
        in_specs=(P(("row", "col"), None, None, None), P(("row", "col"), None)),
        out_specs=P(("row", "col"), None, None, None),
        check_vma=False,
    )
```

```python
import jax
import jax.numpy as jnp
from jax import lax
from jax.experimental import pallas as pl
from jax.experimental.pallas import tpu as pltpu
from jax.sharding import PartitionSpec as P

F32, BF16 = jnp.float32, jnp.bfloat16
MESH = pl.DeviceIdType.MESH
B = 512
H = B // 2
OWN = 2
SLOTS = 5
SPAN = 6
MIB = 2**20
FACTOR = 0.5 / (SLOTS * B)
CORNER = ((2, 2), (2, 3), (3, 3))
INSIDE = [(row, col) for row in (2, 3) for col in range(row - 2, row + 3)]
EARLY = [(2, 0), (2, 1), (2, 2), (2, 3), (2, 4), (3, 1), (3, 2)]
LATE = [(3, 3), (3, 4), (3, 5)]


def chain(step):
    rows, cols = lax.axis_size("row"), lax.axis_size("col")
    place = lax.axis_index("row") * cols + lax.axis_index("col")
    other = lax.rem(place + (step + rows * cols), rows * cols)
    return {"row": lax.div(other, cols), "col": lax.rem(other, cols)}


def at(ref, row, col, height=1, width=1):
    return ref.at[row * B : (row + height) * B, col * B : (col + width) * B]


def product(left, right):
    return jnp.dot(left, right, preferred_element_type=F32)


def over(first, last, body):
    def step(n, carry):
        body(n, pl.multiple_of(n * B, B))
        return carry

    lax.fori_loop(first, last, step, 0)


def ramps():
    row = lax.broadcasted_iota(jnp.int32, (H, H), 0)
    col = lax.broadcasted_iota(jnp.int32, (H, H), 1)
    return row, col


def pack(block, piece):
    row, col = ramps()
    first, second = block[:H, :H].astype(F32), block[H:, H:].astype(F32)
    piece[:H, :H] = jnp.where(row <= col, first, second).astype(BF16)
    diagonal = jnp.sum(jnp.where(row == col, second, 0.0), axis=0, keepdims=True)
    piece[H:, :H] = jnp.broadcast_to(diagonal, (16, H)).astype(BF16)
    piece[H:, H:] = jnp.zeros((16, H), BF16)
    piece[:H, H:] = block[:H, H:]


def unpack(piece, block):
    row, col = ramps()
    tile = piece[:H, :H].astype(F32)
    turned = tile.T
    diagonal = piece[H : H + 16, :H].astype(F32)[:1]
    block[:H, :H] = jnp.where(row <= col, tile, turned).astype(BF16)
    block[H:, H:] = jnp.where(row > col, tile, jnp.where(row < col, turned, diagonal)).astype(BF16)
    side = piece[:H, H:]
    block[:H, H:] = side
    block[H:, :H] = side.T


def kernel(
    band, occupancy, done, base, last_square, last_rows,
    x, s, total, partial, packed, low, high,
    load_sem, send_sem, recv_sem,
):
    after, before = chain(1), chain(-1)
    barrier = pltpu.get_barrier_semaphore()
    for neighbour in (after, before):
        pl.semaphore_signal(barrier, inc=1, device_id=neighbour, device_id_type=MESH)

    def keep(row, col):
        return occupancy[row - OWN, col - (row - OWN)].astype(F32)

    order = [(2, 3), (3, 3), (2, 2)]
    order += [pair for pair in INSIDE if pair not in order]
    loads = {}
    for n, (row, col) in enumerate(order):
        loads[row, col] = pltpu.make_async_copy(
            band.at[row - 2, col - (row - 2)], at(x, row, col), load_sem.at[n]
        )
        loads[row, col].start()

    def loaded(row, col):
        loads[row, col].wait()
        block = at(x, row, col)
        block[...] = (block[...].astype(F32) * keep(row, col)).astype(BF16)

    sources = [packed.at[0], at(x, 2, 3), packed.at[1]]
    landings = [[low.at[0], at(x, 0, 1), low.at[1]], [high.at[0], at(x, 4, 5), high.at[1]]]
    copies = {}

    def send(side, n):
        copies[side, n] = pltpu.make_async_remote_copy(
            src_ref=sources[n],
            dst_ref=landings[side][n],
            send_sem=send_sem.at[side, n],
            recv_sem=recv_sem.at[side, n],
            device_id=(after, before)[side],
            device_id_type=MESH,
        )
        copies[side, n].start()

    loaded(2, 3)
    pl.semaphore_wait(barrier, 2)
    send(0, 1)
    loaded(3, 3)
    pack(at(x, 3, 3), packed.at[1])
    send(0, 2)
    loaded(2, 2)
    pack(at(x, 2, 2), packed.at[0])
    send(0, 0)

    for pair in order[3:]:
        loaded(*pair)
    for row, col in ((2, 0), (2, 1), (3, 1), (2, 4), (3, 4), (3, 5)):
        at(x, col, row)[...] = at(x, row, col)[...].T

    def square(row, col, first, last):
        value = product(at(x, row, first, 1, last - first)[...], at(x, first, col, last - first, 1)[...])
        at(s, row - 2, col)[...] = (value * keep(row, col)).astype(BF16)

    square(2, 2, 0, 5)
    square(3, 3, 1, 6)
    square(2, 3, 1, 5)
    at(s, 1, 2)[...] = at(s, 0, 3)[...].T

    def local(n, c):
        total[:, pl.ds(c, B)] = product(at(s, 0, 2, 2, 2)[...], x[2 * B : 4 * B, pl.ds(c, B)])

    over(1, 5, local)
    at(total, 0, 0)[...] = product(at(s, 0, 2)[...], at(x, 2, 0)[...])
    at(total, 1, 5)[...] = product(at(s, 1, 3)[...], at(x, 3, 5)[...])
    partial[:, :B] = product(at(x, 2, 2, 2, 2)[...], at(x, 2, 4, 2, 1)[...])
    partial[B:, B:] = product(at(x, 3, 3)[...], at(x, 3, 5)[...])

    def finish(row, col, value):
        scale = keep(row, col) * FACTOR
        block = 1.5 * at(x, row, col)[...].astype(F32) - scale * value
        if (row, col) in LATE:
            base[:, (col - 3) * B : (col - 2) * B] = block
        else:
            done[row - 2, col - (row - 2)] = block.astype(BF16)

    for n in (1, 2, 0):
        copies[0, n].wait_send()
    for n in range(3):
        send(1, n)
    copies[0, 1].wait_recv()
    at(x, 1, 0)[...] = at(x, 0, 1)[...].T
    copies[0, 2].wait_recv()
    unpack(low.at[1], at(x, 1, 1))
    square(2, 1, 0, 4)
    square(3, 1, 1, 4)
    copies[0, 0].wait_recv()
    unpack(low.at[0], at(x, 0, 0))
    square(2, 0, 0, 3)
    finish(2, 0, at(total, 0, 0)[...] + product(at(s, 0, 0, 1, 2)[...], at(x, 0, 0, 2, 1)[...]))
    finish(2, 1, at(total, 0, 1)[...] + product(at(s, 0, 0, 1, 2)[...], at(x, 0, 1, 2, 1)[...]))
    at(total, 0, 2)[...] += product(at(s, 0, 0, 1, 2)[...], at(x, 0, 2, 2, 1)[...])
    at(total, 0, 3)[...] += product(at(s, 0, 1)[...], at(x, 1, 3)[...])
    finish(3, 1, at(total, 1, 1)[...] + product(at(s, 1, 1)[...], at(x, 1, 1)[...]))
    for col in (2, 3):
        at(total, 1, col)[...] += product(at(s, 1, 1)[...], at(x, 1, col)[...])

    copies[1, 0].wait_recv()
    unpack(high.at[0], at(x, 4, 4))
    value = partial[:, :B] + product(at(x, 2, 4, 2, 1)[...], at(x, 4, 4)[...])
    at(s, 0, 4)[...] = (value[:B] * keep(2, 4)).astype(BF16)
    partial[B:, :B] = value[B:]
    for col in (2, 3, 4):
        finish(2, col, at(total, 0, col)[...] + product(at(s, 0, 4)[...], at(x, 4, col)[...]))
    copies[1, 1].wait_recv()
    at(x, 5, 4)[...] = at(x, 4, 5)[...].T
    value = partial[B:, :B] + product(at(x, 3, 5)[...], at(x, 5, 4)[...])
    at(s, 1, 4)[...] = (value * keep(3, 4)).astype(BF16)
    for col in (2, 3, 4, 5):
        finish(3, col, at(total, 1, col)[...] + product(at(s, 1, 4)[...], at(x, 4, col)[...]))
    partial[B:, B:] += product(at(x, 3, 4)[...], at(x, 4, 5)[...])
    last_rows[:, : 2 * B] = at(x, 5, 3, 1, 2)[...]
    copies[1, 2].wait_recv()
    unpack(high.at[1], last_rows.at[:, 2 * B :])
    value = partial[B:, B:] + product(at(x, 3, 5)[...], last_rows[:, 2 * B :])
    last_square[...] = (value * keep(3, 5)).astype(BF16)
    for n in range(3):
        copies[1, n].wait_send()


def tail(occupancy, done, base, last_square, last_rows, out, late, store_sem):
    stores = []

    def store(source, row, col):
        place = (row - 2, col - (row - 2))
        copy = pltpu.make_async_copy(source, out.at[place], store_sem.at[place])
        copy.start()
        stores.append(copy)

    for row, col in EARLY:
        store(done.at[row - 2, col - (row - 2)], row, col)
    for n, (row, col) in enumerate(LATE):
        scale = occupancy[row - 2, col - (row - 2)].astype(F32) * FACTOR
        value = product(last_square[...], last_rows[:, n * B : (n + 1) * B])
        late[n] = (base[:, n * B : (n + 1) * B] - scale * value).astype(BF16)
        store(late.at[n], row, col)
    for copy in stores:
        copy.wait()


def on_device(band_blocks, occupancy):
    dma = pltpu.SemaphoreType.DMA
    vmem = pl.BlockSpec(memory_space=pltpu.VMEM)
    smem = pl.BlockSpec(memory_space=pltpu.SMEM)
    hbm = pl.BlockSpec(memory_space=pl.ANY)
    held = pl.pallas_call(
        kernel,
        out_shape=(
            pltpu.VMEM(band_blocks.shape, BF16),
            pltpu.VMEM((B, 3 * B), F32),
            pltpu.VMEM((B, B), BF16),
            pltpu.VMEM((B, 3 * B), BF16),
        ),
        in_specs=[hbm, smem],
        out_specs=(vmem,) * 4,
        scratch_shapes=[
            pltpu.VMEM((SPAN * B, SPAN * B), BF16),
            pltpu.VMEM((OWN * B, SPAN * B), BF16),
            pltpu.VMEM((OWN * B, SPAN * B), F32),
            pltpu.VMEM((OWN * B, 2 * B), F32),
            pltpu.VMEM((2, H + 16, B), BF16),
            pltpu.VMEM((2, H + 16, B), BF16),
            pltpu.VMEM((2, H + 16, B), BF16),
            dma((OWN * SLOTS,)),
            dma((2, 3)),
            dma((2, 3)),
        ],
        compiler_params=pltpu.CompilerParams(
            collective_id=0, has_side_effects=True, vmem_limit_bytes=48 * MIB
        ),
        name="step",
    )(band_blocks, occupancy)
    return pl.pallas_call(
        tail,
        out_shape=jax.ShapeDtypeStruct(band_blocks.shape, BF16),
        in_specs=[smem] + [vmem] * 4,
        out_specs=hbm,
        scratch_shapes=[pltpu.VMEM((3, B, B), BF16), dma((OWN, SLOTS))],
        compiler_params=pltpu.CompilerParams(vmem_limit_bytes=12 * MIB),
        name="finish",
    )(occupancy, *held)


def solution(mesh):
    return jax.shard_map(
        on_device,
        mesh=mesh,
        in_specs=(P(("row", "col"), None, None, None), P(("row", "col"), None)),
        out_specs=P(("row", "col"), None, None, None),
        check_vma=False,
    )
```

```python
import jax
import jax.numpy as jnp
from jax import lax
from jax.experimental import pallas as pl
from jax.experimental.pallas import tpu as pltpu
from jax.sharding import PartitionSpec as P

F32, BF16 = jnp.float32, jnp.bfloat16
MESH = pl.DeviceIdType.MESH
B = 512
H = B // 2
OWN = 2
SLOTS = 5
SPAN = 6
MIB = 2**20
FACTOR = 0.5 / (SLOTS * B)
CORNER = ((2, 2), (2, 3), (3, 3))
INSIDE = [(row, col) for row in (2, 3) for col in range(row - 2, row + 3)]
EARLY = [(2, 0), (2, 1), (2, 2), (2, 3), (2, 4), (3, 1), (3, 2)]
LATE = [(3, 3), (3, 4), (3, 5)]


def chain(step):
    rows, cols = lax.axis_size("row"), lax.axis_size("col")
    place = lax.axis_index("row") * cols + lax.axis_index("col")
    other = lax.rem(place + (step + rows * cols), rows * cols)
    return {"row": lax.div(other, cols), "col": lax.rem(other, cols)}


def at(ref, row, col, height=1, width=1):
    return ref.at[row * B : (row + height) * B, col * B : (col + width) * B]


def product(left, right):
    return jnp.dot(left, right, preferred_element_type=F32)


def over(first, last, body):
    def step(n, carry):
        body(n, pl.multiple_of(n * B, B))
        return carry

    lax.fori_loop(first, last, step, 0)


def ramps():
    row = lax.broadcasted_iota(jnp.int32, (H, H), 0)
    col = lax.broadcasted_iota(jnp.int32, (H, H), 1)
    return row, col


def pack(block, tile):
    row, col = ramps()
    first, second = block[:H, :H].astype(F32), block[H:, H:].astype(F32)
    tile[...] = jnp.where(row <= col, first, second).astype(BF16)
    diagonal = jnp.sum(jnp.where(row == col, second, 0.0), axis=0, keepdims=True)
    return [diagonal[:, : H // 2], diagonal[:, H // 2 :]]


def unpack_side(side, block):
    block[:H, H:] = side[...]
    block[H:, :H] = side[...].T


def unpack(tile, diagonals, n, block):
    row, col = ramps()
    tile = tile[...].astype(F32)
    turned = tile.T
    lines = diagonals[...].astype(F32)
    diagonal = jnp.concatenate([lines[2 * n : 2 * n + 1], lines[2 * n + 1 : 2 * n + 2]], axis=1)
    block[:H, :H] = jnp.where(row <= col, tile, turned).astype(BF16)
    block[H:, H:] = jnp.where(row > col, tile, jnp.where(row < col, turned, diagonal)).astype(BF16)


def kernel(
    band, occupied, done, base, part_square, left, last_rows, last_side, last_tile, last_diagonals,
    x, s, total, partial, packed, diagonals, low, low_diagonals, high,
    occupancy, load_sem, send_sem, recv_sem, ready,
):
    after, before = chain(1), chain(-1)
    barrier = pltpu.get_barrier_semaphore()
    pl.semaphore_signal(barrier, inc=1, device_id=before, device_id_type=MESH)

    def keep(row, col):
        return occupancy[row - OWN, col - (row - OWN)].astype(F32)

    order = [(2, 3), (3, 3), (2, 2)]
    order += [pair for pair in INSIDE if pair not in order]
    loads = {}
    for n, (row, col) in enumerate(order):
        loads[row, col] = pltpu.make_async_copy(
            band.at[row - 2, col - (row - 2)], at(x, row, col), load_sem.at[n]
        )
        loads[row, col].start()

    flags = pltpu.make_async_copy(occupied, occupancy, load_sem.at[len(order)])
    flags.start()

    def loaded(row, col):
        loads[row, col].wait()
        block = at(x, row, col)
        block[...] = (block[...].astype(F32) * keep(row, col)).astype(BF16)

    sources = [packed.at[0], packed.at[1], at(x, 2, 3), diagonals, band.at[0, 2, :H, H:], band.at[1, 2, :H, H:]]
    landings = [
        [low.at[0], low.at[1], at(x, 0, 1), low_diagonals, low.at[2], low.at[3]],
        [high.at[0], last_tile, at(x, 4, 5), last_diagonals, high.at[1], last_side],
    ]
    copies = {}

    for side in range(2):
        for n in range(6):
            copies[side, n] = pltpu.make_async_remote_copy(
                src_ref=sources[n],
                dst_ref=landings[side][n],
                send_sem=send_sem.at[side, n],
                recv_sem=recv_sem.at[side, n],
                device_id=(after, before)[side],
                device_id_type=MESH,
            )

    def send(side, n):
        copies[side, n].start()

    pl.semaphore_wait(barrier, 1)
    for n in (5, 4):
        send(0, n)
    pl.semaphore_signal(ready, inc=1, device_id=after, device_id_type=MESH)
    flags.wait()
    loaded(2, 3)
    send(0, 2)
    loaded(3, 3)
    second = pack(at(x, 3, 3), packed.at[1])
    loaded(2, 2)
    first = pack(at(x, 2, 2), packed.at[0])
    diagonals[...] = jnp.concatenate(first + second + [jnp.zeros((12, H // 2), F32)], axis=0).astype(BF16)
    for n in (3, 1, 0):
        send(0, n)

    for pair in order[3:]:
        loaded(*pair)
    for row, col in ((2, 0), (2, 1), (3, 1), (2, 4), (3, 4), (3, 5)):
        at(x, col, row)[...] = at(x, row, col)[...].T

    last_in_run = lax.axis_index("col") == lax.axis_size("col") - 1

    def send_before():
        for n in (4, 3, 0, 2, 5, 1):
            send(1, n)

    def square(row, col, first, last):
        value = product(at(x, row, first, 1, last - first)[...], at(x, first, col, last - first, 1)[...])
        at(s, row - 2, col)[...] = (value * keep(row, col)).astype(BF16)

    square(2, 2, 0, 5)
    square(3, 3, 1, 6)
    pl.semaphore_wait(ready, 1)

    @pl.when(jnp.logical_not(last_in_run))
    def _():
        send_before()

    square(2, 3, 1, 5)
    at(s, 1, 2)[...] = at(s, 0, 3)[...].T

    def local(n, c):
        total[:, pl.ds(c, B)] = product(at(s, 0, 2, 2, 2)[...], x[2 * B : 4 * B, pl.ds(c, B)])

    over(1, 5, local)
    at(total, 0, 0)[...] = product(at(s, 0, 2)[...], at(x, 2, 0)[...])
    at(total, 1, 5)[...] = product(at(s, 1, 3)[...], at(x, 3, 5)[...])
    partial[:, :B] = product(at(x, 2, 2, 2, 2)[...], at(x, 2, 4, 2, 1)[...])
    partial[B:, B:] = product(at(x, 3, 3)[...], at(x, 3, 5)[...])

    def finish(row, col, value):
        scale = keep(row, col) * FACTOR
        block = 1.5 * at(x, row, col)[...].astype(F32) - scale * value
        if (row, col) in LATE:
            base[:, (col - 3) * B : (col - 2) * B] = block
        else:
            done[row - 2, col - (row - 2)] = block.astype(BF16)

    @pl.when(last_in_run)
    def _():
        for n in range(6):
            copies[0, n].wait_send()
        send_before()

    def near_corner():
        copies[1, 4].wait_recv()
        unpack_side(high.at[1], at(x, 4, 4))
        copies[1, 3].wait_recv()
        copies[1, 0].wait_recv()
        unpack(high.at[0], last_diagonals, 0, at(x, 4, 4))
        value = partial[:, :B] + product(at(x, 2, 4, 2, 1)[...], at(x, 4, 4)[...])
        at(s, 0, 4)[...] = (value[:B] * keep(2, 4)).astype(BF16)
        partial[B:, :B] = value[B:]
        for col in (2, 3):
            at(total, 0, col)[...] += product(at(s, 0, 4)[...], at(x, 4, col)[...])
        finish(2, 4, at(total, 0, 4)[...] + product(at(s, 0, 4)[...], at(x, 4, 4)[...]))

    first_in_run = lax.axis_index("col") == 0
    pl.when(first_in_run)(near_corner)

    copies[0, 5].wait_recv()
    unpack_side(low.at[3], at(x, 1, 1))
    copies[0, 4].wait_recv()
    unpack_side(low.at[2], at(x, 0, 0))
    copies[0, 2].wait_recv()
    at(x, 1, 0)[...] = at(x, 0, 1)[...].T
    copies[0, 3].wait_recv()
    copies[0, 1].wait_recv()
    unpack(low.at[1], low_diagonals, 1, at(x, 1, 1))
    square(2, 1, 0, 4)
    square(3, 1, 1, 4)
    copies[0, 0].wait_recv()
    unpack(low.at[0], low_diagonals, 0, at(x, 0, 0))
    square(2, 0, 0, 3)
    finish(2, 0, at(total, 0, 0)[...] + product(at(s, 0, 0, 1, 2)[...], at(x, 0, 0, 2, 1)[...]))
    finish(2, 1, at(total, 0, 1)[...] + product(at(s, 0, 0, 1, 2)[...], at(x, 0, 1, 2, 1)[...]))
    at(total, 0, 2)[...] += product(at(s, 0, 0, 1, 2)[...], at(x, 0, 2, 2, 1)[...])
    at(total, 0, 3)[...] += product(at(s, 0, 1)[...], at(x, 1, 3)[...])
    finish(3, 1, at(total, 1, 1)[...] + product(at(s, 1, 1)[...], at(x, 1, 1)[...]))
    for col in (2, 3):
        at(total, 1, col)[...] += product(at(s, 1, 1)[...], at(x, 1, col)[...])

    pl.when(jnp.logical_not(first_in_run))(near_corner)
    for col in (2, 3):
        finish(2, col, at(total, 0, col)[...])

    copies[1, 2].wait_recv()
    at(x, 5, 4)[...] = at(x, 4, 5)[...].T
    value = partial[B:, :B] + product(at(x, 3, 5)[...], at(x, 5, 4)[...])
    at(s, 1, 4)[...] = (value * keep(3, 4)).astype(BF16)
    for col in (2, 3, 4, 5):
        finish(3, col, at(total, 1, col)[...] + product(at(s, 1, 4)[...], at(x, 4, col)[...]))
    value = partial[B:, B:] + product(at(x, 3, 4)[...], at(x, 4, 5)[...])
    last_rows[...] = at(x, 5, 3, 1, 2)[...]
    left[...] = at(x, 3, 5)[...]
    copies[1, 5].wait_recv()
    part_square[:, :H] = value[:, :H] + product(left[:, H:], last_side[...].T)
    part_square[:, H:] = value[:, H:] + product(left[:, :H], last_side[...])
    copies[1, 1].wait_recv()
    for n in range(6):
        copies[1, n].wait_send()

    @pl.when(jnp.logical_not(last_in_run))
    def _():
        for n in range(6):
            copies[0, n].wait_send()


def tail(occupancy, done, base, part_square, left, last_rows, last_side, last_tile, last_diagonals, out, corner, late, store_sem):
    stores = []

    def store(source, row, col):
        place = (row - 2, col - (row - 2))
        copy = pltpu.make_async_copy(source, out.at[place], store_sem.at[place])
        copy.start()
        stores.append(copy)

    for row, col in EARLY:
        store(done.at[row - 2, col - (row - 2)], row, col)
    unpack_side(last_side, corner)
    unpack(last_tile, last_diagonals, 1, corner)
    squares = []
    for half in (slice(0, H), slice(H, B)):
        value = part_square[:, half] + product(left[:, half], corner[half, half])
        squares.append((value * occupancy[1, 4].astype(F32)).astype(BF16))
    square = jnp.concatenate(squares, axis=1)
    rows = [last_rows.at[:, :B], last_rows.at[:, B:], corner]
    for n, (row, col) in enumerate(LATE):
        scale = occupancy[row - 2, col - (row - 2)].astype(F32) * FACTOR
        value = product(square, rows[n][...])
        late[n] = (base[:, n * B : (n + 1) * B] - scale * value).astype(BF16)
        store(late.at[n], row, col)
    for copy in stores:
        copy.wait()


def on_device(band_blocks, occupancy):
    dma = pltpu.SemaphoreType.DMA
    vmem = pl.BlockSpec(memory_space=pltpu.VMEM)
    smem = pl.BlockSpec(memory_space=pltpu.SMEM)
    hbm = pl.BlockSpec(memory_space=pl.ANY)
    held = pl.pallas_call(
        kernel,
        out_shape=(
            pltpu.VMEM(band_blocks.shape, BF16),
            pltpu.VMEM((B, 3 * B), F32),
            pltpu.VMEM((B, B), F32),
            pltpu.VMEM((B, B), BF16),
            pltpu.VMEM((B, 2 * B), BF16),
            pltpu.VMEM((H, H), BF16),
            pltpu.VMEM((H, H), BF16),
            pltpu.VMEM((16, H // 2), BF16),
        ),
        in_specs=[hbm, hbm],
        out_specs=(vmem,) * 8,
        scratch_shapes=[
            pltpu.VMEM((SPAN * B, SPAN * B), BF16),
            pltpu.VMEM((OWN * B, SPAN * B), BF16),
            pltpu.VMEM((OWN * B, SPAN * B), F32),
            pltpu.VMEM((OWN * B, 2 * B), F32),
            pltpu.VMEM((2, H, H), BF16),
            pltpu.VMEM((16, H // 2), BF16),
            pltpu.VMEM((4, H, H), BF16),
            pltpu.VMEM((16, H // 2), BF16),
            pltpu.VMEM((2, H, H), BF16),
            pltpu.SMEM((OWN, SLOTS), jnp.int32),
            dma((OWN * SLOTS + 1,)),
            dma((2, 6)),
            dma((2, 6)),
            pltpu.SemaphoreType.REGULAR,
        ],
        compiler_params=pltpu.CompilerParams(
            collective_id=0, has_side_effects=True, vmem_limit_bytes=48 * MIB
        ),
        name="step",
    )(band_blocks, occupancy)
    return pl.pallas_call(
        tail,
        out_shape=jax.ShapeDtypeStruct(band_blocks.shape, BF16),
        in_specs=[smem] + [vmem] * 8,
        out_specs=hbm,
        scratch_shapes=[pltpu.VMEM((B, B), BF16), pltpu.VMEM((3, B, B), BF16), dma((OWN, SLOTS))],
        compiler_params=pltpu.CompilerParams(vmem_limit_bytes=12 * MIB),
        name="finish",
    )(occupancy, *held)


def solution(mesh):
    return jax.shard_map(
        on_device,
        mesh=mesh,
        in_specs=(P(("row", "col"), None, None, None), P(("row", "col"), None)),
        out_specs=P(("row", "col"), None, None, None),
        check_vma=False,
    )
```

```python
import jax
import jax.numpy as jnp
from jax import lax
from jax.experimental import pallas as pl
from jax.experimental.pallas import tpu as pltpu
from jax.sharding import PartitionSpec as P

F32, BF16 = jnp.float32, jnp.bfloat16
MESH = pl.DeviceIdType.MESH
B = 512
H = B // 2
OWN = 2
SLOTS = 5
SPAN = 6
MIB = 2**20
FACTOR = 0.5 / (SLOTS * B)
CORNER = ((2, 2), (2, 3), (3, 3))
INSIDE = [(row, col) for row in (2, 3) for col in range(row - 2, row + 3)]
EARLY = [(2, 0), (2, 1), (2, 2), (2, 3), (2, 4), (3, 1), (3, 2)]
LATE = [(3, 3), (3, 4), (3, 5)]


def chain(step):
    rows, cols = lax.axis_size("row"), lax.axis_size("col")
    place = lax.axis_index("row") * cols + lax.axis_index("col")
    other = lax.rem(place + (step + rows * cols), rows * cols)
    return {"row": lax.div(other, cols), "col": lax.rem(other, cols)}


def at(ref, row, col, height=1, width=1):
    return ref.at[row * B : (row + height) * B, col * B : (col + width) * B]


def product(left, right):
    return jnp.dot(left, right, preferred_element_type=F32)


def over(first, last, body):
    def step(n, carry):
        body(n, pl.multiple_of(n * B, B))
        return carry

    lax.fori_loop(first, last, step, 0)


def ramps():
    row = lax.broadcasted_iota(jnp.int32, (H, H), 0)
    col = lax.broadcasted_iota(jnp.int32, (H, H), 1)
    return row, col


def pack(block, tile):
    row, col = ramps()
    first, second = block[:H, :H].astype(F32), block[H:, H:].astype(F32)
    tile[...] = jnp.where(row <= col, first, second).astype(BF16)
    diagonal = jnp.sum(jnp.where(row == col, second, 0.0), axis=0, keepdims=True)
    return [diagonal[:, : H // 2], diagonal[:, H // 2 :]]


def unpack_side(side, block):
    block[:H, H:] = side[...]
    block[H:, :H] = side[...].T


def unpack(tile, diagonals, n, block):
    row, col = ramps()
    tile = tile[...].astype(F32)
    turned = tile.T
    lines = diagonals[...].astype(F32)
    diagonal = jnp.concatenate([lines[2 * n : 2 * n + 1], lines[2 * n + 1 : 2 * n + 2]], axis=1)
    block[:H, :H] = jnp.where(row <= col, tile, turned).astype(BF16)
    block[H:, H:] = jnp.where(row > col, tile, jnp.where(row < col, turned, diagonal)).astype(BF16)


def kernel(
    band, occupied, done, base, part_square, left, last_rows, last_side, last_tile, last_diagonals,
    x, s, total, partial, packed, diagonals, low, low_diagonals, high,
    occupancy, load_sem, send_sem, recv_sem, ready,
):
    after, before = chain(1), chain(-1)
    place, last = lax.axis_index("col"), lax.axis_size("col") - 1
    first_in_run, last_in_run = place == 0, place == last
    inside_run = jnp.logical_not(jnp.logical_or(first_in_run, last_in_run))

    def signal(semaphore, device):
        pl.semaphore_signal(semaphore, inc=1, device_id=device, device_id_type=MESH)

    barrier = pltpu.get_barrier_semaphore()

    @pl.when(jnp.logical_not(last_in_run))
    def _():
        signal(barrier, after)

    @pl.when(place <= 1)
    def _():
        signal(barrier, before)


    def keep(row, col):
        return occupancy[row - OWN, col - (row - OWN)].astype(F32)

    order = [(2, 3), (3, 3), (2, 2)]
    order += [pair for pair in INSIDE if pair not in order]
    loads = {}
    for n, (row, col) in enumerate(order):
        loads[row, col] = pltpu.make_async_copy(
            band.at[row - 2, col - (row - 2)], at(x, row, col), load_sem.at[n]
        )
        loads[row, col].start()

    flags = pltpu.make_async_copy(occupied, occupancy, load_sem.at[len(order)])
    flags.start()

    def loaded(row, col):
        loads[row, col].wait()
        block = at(x, row, col)
        block[...] = (block[...].astype(F32) * keep(row, col)).astype(BF16)

    sources = [packed.at[0], packed.at[1], at(x, 2, 3), diagonals, band.at[0, 2, :H, H:], band.at[1, 2, :H, H:]]
    landings = [
        [low.at[0], low.at[1], at(x, 0, 1), low_diagonals, low.at[2], low.at[3]],
        [high.at[0], last_tile, at(x, 4, 5), last_diagonals, high.at[1], last_side],
    ]
    copies = {}

    for side in range(2):
        for n in range(6):
            copies[side, n] = pltpu.make_async_remote_copy(
                src_ref=sources[n],
                dst_ref=landings[side][n],
                send_sem=send_sem.at[side, n],
                recv_sem=recv_sem.at[side, n],
                device_id=(after, before)[side],
                device_id_type=MESH,
            )

    def send(side, n):
        copies[side, n].start()


    @pl.when(last_in_run)
    def _():
        pl.semaphore_wait(barrier, 2)

    @pl.when(jnp.logical_not(last_in_run))
    def _():
        pl.semaphore_wait(barrier, 1)

    @pl.when(inside_run)
    def _():
        send(1, 4)

    @pl.when(place >= 2)
    def _():
        signal(ready, before)

    @pl.when(last_in_run)
    def _():
        signal(ready, after)

    @pl.when(inside_run)
    def _():
        pl.semaphore_wait(ready, 1)

    for n in (5, 4):
        send(0, n)
    flags.wait()
    loaded(2, 3)
    send(0, 2)
    loaded(3, 3)
    second = pack(at(x, 3, 3), packed.at[1])
    loaded(2, 2)
    first = pack(at(x, 2, 2), packed.at[0])
    diagonals[...] = jnp.concatenate(first + second + [jnp.zeros((12, H // 2), F32)], axis=0).astype(BF16)
    for n in (3, 1, 0):
        send(0, n)

    for pair in order[3:]:
        loaded(*pair)
    for row, col in ((2, 0), (2, 1), (3, 1), (2, 4), (3, 4), (3, 5)):
        at(x, col, row)[...] = at(x, row, col)[...].T

    def send_before():
        for n in (3, 0, 2, 5, 1):
            send(1, n)

    def square(row, col, first, last):
        value = product(at(x, row, first, 1, last - first)[...], at(x, first, col, last - first, 1)[...])
        at(s, row - 2, col)[...] = (value * keep(row, col)).astype(BF16)

    square(2, 2, 0, 5)
    square(3, 3, 1, 6)

    @pl.when(first_in_run)
    def _():
        pl.semaphore_wait(ready, 1)
        send(1, 4)

    @pl.when(jnp.logical_not(last_in_run))
    def _():
        send_before()

    square(2, 3, 1, 5)
    at(s, 1, 2)[...] = at(s, 0, 3)[...].T

    def local(n, c):
        total[:, pl.ds(c, B)] = product(at(s, 0, 2, 2, 2)[...], x[2 * B : 4 * B, pl.ds(c, B)])

    over(1, 5, local)
    at(total, 0, 0)[...] = product(at(s, 0, 2)[...], at(x, 2, 0)[...])
    at(total, 1, 5)[...] = product(at(s, 1, 3)[...], at(x, 3, 5)[...])
    partial[:, :B] = product(at(x, 2, 2, 2, 2)[...], at(x, 2, 4, 2, 1)[...])
    partial[B:, B:] = product(at(x, 3, 3)[...], at(x, 3, 5)[...])
    part20, part21, part31 = partial.at[:B, B:], at(total, 0, 5), at(total, 1, 0)
    part20[...] = product(at(x, 2, 2)[...], at(x, 2, 0)[...])
    value = product(at(x, 2, 2, 2, 2)[...], at(x, 2, 1, 2, 1)[...])
    part21[...] = value[:B]
    part31[...] = value[B:]

    def finish(row, col, value):
        scale = keep(row, col) * FACTOR
        block = 1.5 * at(x, row, col)[...].astype(F32) - scale * value
        if (row, col) in LATE:
            base[:, (col - 3) * B : (col - 2) * B] = block
        else:
            done[row - 2, col - (row - 2)] = block.astype(BF16)

    @pl.when(last_in_run)
    def _():
        for n in range(6):
            copies[0, n].wait_send()
        send(1, 4)
        send_before()

    def near_corner():
        copies[1, 4].wait_recv()
        unpack_side(high.at[1], at(x, 4, 4))
        copies[1, 3].wait_recv()
        copies[1, 0].wait_recv()
        unpack(high.at[0], last_diagonals, 0, at(x, 4, 4))
        value = partial[:, :B] + product(at(x, 2, 4, 2, 1)[...], at(x, 4, 4)[...])
        at(s, 0, 4)[...] = (value[:B] * keep(2, 4)).astype(BF16)
        partial[B:, :B] = value[B:]
        for col in (2, 3):
            at(total, 0, col)[...] += product(at(s, 0, 4)[...], at(x, 4, col)[...])
        finish(2, 4, at(total, 0, 4)[...] + product(at(s, 0, 4)[...], at(x, 4, 4)[...]))

    pl.when(first_in_run)(near_corner)

    copies[0, 5].wait_recv()
    unpack_side(low.at[3], at(x, 1, 1))
    copies[0, 4].wait_recv()
    unpack_side(low.at[2], at(x, 0, 0))
    copies[0, 2].wait_recv()
    at(x, 1, 0)[...] = at(x, 0, 1)[...].T
    part20[...] += product(at(x, 2, 1)[...], at(x, 1, 0)[...])
    part21[...] += product(at(x, 2, 0)[...], at(x, 0, 1)[...])
    copies[0, 3].wait_recv()
    copies[0, 1].wait_recv()
    unpack(low.at[1], low_diagonals, 1, at(x, 1, 1))
    at(s, 0, 1)[...] = ((part21[...] + product(at(x, 2, 1)[...], at(x, 1, 1)[...])) * keep(2, 1)).astype(BF16)
    at(s, 1, 1)[...] = ((part31[...] + product(at(x, 3, 1)[...], at(x, 1, 1)[...])) * keep(3, 1)).astype(BF16)
    at(total, 0, 3)[...] += product(at(s, 0, 1)[...], at(x, 1, 3)[...])
    finish(3, 1, at(total, 1, 1)[...] + product(at(s, 1, 1)[...], at(x, 1, 1)[...]))
    for col in (2, 3):
        at(total, 1, col)[...] += product(at(s, 1, 1)[...], at(x, 1, col)[...])
    copies[0, 0].wait_recv()
    unpack(low.at[0], low_diagonals, 0, at(x, 0, 0))
    at(s, 0, 0)[...] = ((part20[...] + product(at(x, 2, 0)[...], at(x, 0, 0)[...])) * keep(2, 0)).astype(BF16)
    finish(2, 0, at(total, 0, 0)[...] + product(at(s, 0, 0, 1, 2)[...], at(x, 0, 0, 2, 1)[...]))
    finish(2, 1, at(total, 0, 1)[...] + product(at(s, 0, 0, 1, 2)[...], at(x, 0, 1, 2, 1)[...]))
    at(total, 0, 2)[...] += product(at(s, 0, 0, 1, 2)[...], at(x, 0, 2, 2, 1)[...])

    pl.when(jnp.logical_not(first_in_run))(near_corner)
    for col in (2, 3):
        finish(2, col, at(total, 0, col)[...])

    copies[1, 2].wait_recv()
    at(x, 5, 4)[...] = at(x, 4, 5)[...].T
    value = partial[B:, :B] + product(at(x, 3, 5)[...], at(x, 5, 4)[...])
    at(s, 1, 4)[...] = (value * keep(3, 4)).astype(BF16)
    for col in (2, 3, 4, 5):
        finish(3, col, at(total, 1, col)[...] + product(at(s, 1, 4)[...], at(x, 4, col)[...]))
    value = partial[B:, B:] + product(at(x, 3, 4)[...], at(x, 4, 5)[...])
    last_rows[...] = at(x, 5, 3, 1, 2)[...]
    left[...] = at(x, 3, 5)[...]
    copies[1, 5].wait_recv()
    part_square[:, :H] = value[:, :H] + product(left[:, H:], last_side[...].T)
    part_square[:, H:] = value[:, H:] + product(left[:, :H], last_side[...])
    copies[1, 1].wait_recv()
    for n in range(6):
        copies[1, n].wait_send()

    @pl.when(jnp.logical_not(last_in_run))
    def _():
        for n in range(6):
            copies[0, n].wait_send()


def tail(occupancy, done, base, part_square, left, last_rows, last_side, last_tile, last_diagonals, out, corner, late, store_sem):
    stores = []

    def store(source, row, col):
        place = (row - 2, col - (row - 2))
        copy = pltpu.make_async_copy(source, out.at[place], store_sem.at[place])
        copy.start()
        stores.append(copy)

    for row, col in EARLY:
        store(done.at[row - 2, col - (row - 2)], row, col)
    unpack_side(last_side, corner)
    unpack(last_tile, last_diagonals, 1, corner)
    squares = []
    for half in (slice(0, H), slice(H, B)):
        value = part_square[:, half] + product(left[:, half], corner[half, half])
        squares.append((value * occupancy[1, 4].astype(F32)).astype(BF16))
    square = jnp.concatenate(squares, axis=1)
    rows = [last_rows.at[:, :B], last_rows.at[:, B:], corner]
    for n, (row, col) in enumerate(LATE):
        scale = occupancy[row - 2, col - (row - 2)].astype(F32) * FACTOR
        value = product(square, rows[n][...])
        late[n] = (base[:, n * B : (n + 1) * B] - scale * value).astype(BF16)
        store(late.at[n], row, col)
    for copy in stores:
        copy.wait()


def on_device(band_blocks, occupancy):
    dma = pltpu.SemaphoreType.DMA
    vmem = pl.BlockSpec(memory_space=pltpu.VMEM)
    smem = pl.BlockSpec(memory_space=pltpu.SMEM)
    hbm = pl.BlockSpec(memory_space=pl.ANY)
    held = pl.pallas_call(
        kernel,
        out_shape=(
            pltpu.VMEM(band_blocks.shape, BF16),
            pltpu.VMEM((B, 3 * B), F32),
            pltpu.VMEM((B, B), F32),
            pltpu.VMEM((B, B), BF16),
            pltpu.VMEM((B, 2 * B), BF16),
            pltpu.VMEM((H, H), BF16),
            pltpu.VMEM((H, H), BF16),
            pltpu.VMEM((16, H // 2), BF16),
        ),
        in_specs=[hbm, hbm],
        out_specs=(vmem,) * 8,
        scratch_shapes=[
            pltpu.VMEM((SPAN * B, SPAN * B), BF16),
            pltpu.VMEM((OWN * B, SPAN * B), BF16),
            pltpu.VMEM((OWN * B, SPAN * B), F32),
            pltpu.VMEM((OWN * B, 2 * B), F32),
            pltpu.VMEM((2, H, H), BF16),
            pltpu.VMEM((16, H // 2), BF16),
            pltpu.VMEM((4, H, H), BF16),
            pltpu.VMEM((16, H // 2), BF16),
            pltpu.VMEM((2, H, H), BF16),
            pltpu.SMEM((OWN, SLOTS), jnp.int32),
            dma((OWN * SLOTS + 1,)),
            dma((2, 6)),
            dma((2, 6)),
            pltpu.SemaphoreType.REGULAR,
        ],
        compiler_params=pltpu.CompilerParams(
            collective_id=0, has_side_effects=True, vmem_limit_bytes=48 * MIB
        ),
        name="step",
    )(band_blocks, occupancy)
    return pl.pallas_call(
        tail,
        out_shape=jax.ShapeDtypeStruct(band_blocks.shape, BF16),
        in_specs=[smem] + [vmem] * 8,
        out_specs=hbm,
        scratch_shapes=[pltpu.VMEM((B, B), BF16), pltpu.VMEM((3, B, B), BF16), dma((OWN, SLOTS))],
        compiler_params=pltpu.CompilerParams(vmem_limit_bytes=12 * MIB),
        name="finish",
    )(occupancy, *held)


def solution(mesh):
    return jax.shard_map(
        on_device,
        mesh=mesh,
        in_specs=(P(("row", "col"), None, None, None), P(("row", "col"), None)),
        out_specs=P(("row", "col"), None, None, None),
        check_vma=False,
    )
```

```python
import jax
import jax.numpy as jnp
from jax import lax
from jax.experimental import pallas as pl
from jax.experimental.pallas import tpu as pltpu
from jax.sharding import PartitionSpec as P

F32, BF16 = jnp.float32, jnp.bfloat16
MESH = pl.DeviceIdType.MESH
B = 512
H = B // 2
OWN = 2
SLOTS = 5
SPAN = 6
MIB = 2**20
FACTOR = 0.5 / (SLOTS * B)
CORNER = ((2, 2), (2, 3), (3, 3))
PIECES = 9
STRIPS = (2, 3, 4, 5)
OTHERS = (0, 1, 6, 7, 8)
STRIP = B // len(STRIPS)
INSIDE = [(row, col) for row in (2, 3) for col in range(row - 2, row + 3)]
EARLY = [(2, 0), (2, 1), (2, 2), (2, 3), (2, 4), (3, 1), (3, 2)]
LATE = [(3, 3), (3, 4), (3, 5)]


def chain(step):
    rows, cols = lax.axis_size("row"), lax.axis_size("col")
    place = lax.axis_index("row") * cols + lax.axis_index("col")
    other = lax.rem(place + (step + rows * cols), rows * cols)
    return {"row": lax.div(other, cols), "col": lax.rem(other, cols)}


def at(ref, row, col, height=1, width=1):
    return ref.at[row * B : (row + height) * B, col * B : (col + width) * B]


def product(left, right):
    return jnp.dot(left, right, preferred_element_type=F32)


def over(first, last, body):
    def step(n, carry):
        body(n, pl.multiple_of(n * B, B))
        return carry

    lax.fori_loop(first, last, step, 0)


def ramps():
    row = lax.broadcasted_iota(jnp.int32, (H, H), 0)
    col = lax.broadcasted_iota(jnp.int32, (H, H), 1)
    return row, col


def pack(block, tile):
    row, col = ramps()
    first, second = block[:H, :H].astype(F32), block[H:, H:].astype(F32)
    tile[...] = jnp.where(row <= col, first, second).astype(BF16)
    diagonal = jnp.sum(jnp.where(row == col, second, 0.0), axis=0, keepdims=True)
    return [diagonal[:, : H // 2], diagonal[:, H // 2 :]]


def unpack_side(side, block):
    block[:H, H:] = side[...]
    block[H:, :H] = side[...].T


def unpack(tile, diagonals, n, block):
    row, col = ramps()
    tile = tile[...].astype(F32)
    turned = tile.T
    lines = diagonals[...].astype(F32)
    diagonal = jnp.concatenate([lines[2 * n : 2 * n + 1], lines[2 * n + 1 : 2 * n + 2]], axis=1)
    block[:H, :H] = jnp.where(row <= col, tile, turned).astype(BF16)
    block[H:, H:] = jnp.where(row > col, tile, jnp.where(row < col, turned, diagonal)).astype(BF16)


def kernel(
    band, occupied, done, base, part_square, left, last_rows, last_side, last_tile, last_diagonals,
    x, s, total, partial, packed, diagonals, tiles, sides, lines,
    occupancy, load_sem, send_sem, recv_sem, ready,
):
    place, last = lax.axis_index("col"), lax.axis_size("col") - 1
    parity = lax.rem(place, 2)
    even, odd = parity == 0, parity == 1
    first_in_run, last_in_run = place == 0, place == last
    step = 1 - 2 * parity
    partner, target, origin = chain(step), chain(2 * step), chain(-2 * step)
    low, high = 1 - parity, parity
    cols = last + 1
    odd_run = lax.rem(lax.axis_index("row"), 2) == 1
    even_run = jnp.logical_not(odd_run)
    head, foot = place <= 1, place >= last - 1
    far = jnp.logical_or(jnp.logical_and(odd_run, foot), jnp.logical_and(even_run, head))
    relay = jnp.logical_and(jnp.logical_or(head, foot), jnp.logical_not(far))
    ends = jnp.logical_or(first_in_run, last_in_run)
    crossing = jnp.logical_and(far, ends)
    spared = jnp.logical_and(far, jnp.logical_not(ends))
    other_end = chain(jnp.where(head, last - 1, 1 - last))
    beyond = chain(jnp.where(head, cols - place, last - place - cols))

    def signal(semaphore, device):
        pl.semaphore_signal(semaphore, inc=1, device_id=device, device_id_type=MESH)

    def when(condition, *more):
        for other in more:
            condition = jnp.logical_and(condition, other)
        return pl.when(condition)

    barrier = pltpu.get_barrier_semaphore()
    signal(barrier, partner)

    @when(jnp.logical_not(last_in_run), jnp.logical_not(jnp.logical_and(first_in_run, even_run)))
    def _():
        signal(barrier, origin)

    @when(head)
    def _():
        signal(barrier, other_end)

    @when(place == 1, odd_run)
    def _():
        signal(barrier, chain(-2))

    @when(crossing)
    def _():
        for n in (0, 1):
            signal(barrier, chain(jnp.where(last_in_run, cols - n, n - cols)))

    def keep(row, col):
        return occupancy[row - OWN, col - (row - OWN)].astype(F32)

    order = [(2, 3), (2, 2), (3, 3)]
    order += [pair for pair in INSIDE if pair not in order]
    loads = {}
    for n, (row, col) in enumerate(order):
        loads[row, col] = pltpu.make_async_copy(
            band.at[row - 2, col - (row - 2)], at(x, row, col), load_sem.at[n]
        )
        loads[row, col].start()
    flags = pltpu.make_async_copy(occupied, occupancy, load_sem.at[len(order)])
    flags.start()

    def loaded(row, col):
        loads[row, col].wait()
        block = at(x, row, col)
        block[...] = (block[...].astype(F32) * keep(row, col)).astype(BF16)

    def landing(slot, n):
        if n < 2:
            return tiles.at[slot, n]
        if n < 6:
            return sides.at[slot, (n - 2) * STRIP : (n - 1) * STRIP]
        return lines.at[slot] if n == 6 else tiles.at[slot, n - 5]

    def strip(n):
        return x.at[2 * B + (n - 2) * STRIP : 2 * B + (n - 1) * STRIP, 3 * B : 4 * B]

    sources = [band.at[0, 2, :H, H:], band.at[1, 2, :H, H:]] + [strip(n) for n in STRIPS]
    sources += [diagonals, packed.at[0], packed.at[1]]

    def remote(source, slot, kind, n, device):
        return pltpu.make_async_remote_copy(
            src_ref=source,
            dst_ref=landing(slot, n),
            send_sem=send_sem.at[kind, n],
            recv_sem=recv_sem.at[slot, n],
            device_id=device,
            device_id_type=MESH,
        )

    direct = [remote(sources[n], 0, 0, n, partner) for n in range(PIECES)]
    onward = [remote(landing(0, n), 1, 1, n, target) for n in range(PIECES)]
    aside = {n: remote(landing(0, n), 2, 1, n, other_end) for n in OTHERS}
    across = {n: remote(strip(n), 2, 2, n, other_end) for n in STRIPS}
    relays = [remote(landing(2, n), 1, 2, n, beyond) for n in range(PIECES)]

    def forward(n):
        direct[n].wait_recv()
        when(jnp.logical_not(spared))(onward[n].start)
        if n in OTHERS:
            when(spared)(aside[n].start)

    def pass_on(condition, pieces):
        @when(relay, condition)
        def _():
            for n in pieces:
                across[n].wait_recv() if n in STRIPS else aside[n].wait_recv()
                relays[n].start()

    def arrived(relayed, *pieces):
        @when(relayed)
        def _():
            for n in pieces:
                onward[n].wait_recv()

    for run, counts in ((odd_run, (3, 2, 2, 3)), (even_run, (2, 1, 4, 5))):
        for position, count in zip((0, 1, last - 1, last), counts):

            @when(run, place == position)
            def _():
                pl.semaphore_wait(barrier, count)

    @when(jnp.logical_not(jnp.logical_or(head, foot)))
    def _():
        pl.semaphore_wait(barrier, 2)

    @when(even_run, foot)
    def _():
        signal(ready, other_end)

    @when(even_run, last_in_run)
    def _():
        signal(ready, chain(2))

    direct[0].start()
    direct[1].start()
    flags.wait()
    loaded(2, 3)
    for n in STRIPS:
        direct[n].start()
    loaded(2, 2)
    first = pack(at(x, 2, 2), packed.at[0])
    loaded(3, 3)
    second = pack(at(x, 3, 3), packed.at[1])
    diagonals[...] = jnp.concatenate(first + second + [jnp.zeros((12, H // 2), F32)], axis=0).astype(BF16)
    for n in (6, 7, 8):
        direct[n].start()

    @when(crossing, last_in_run)
    def _():
        for n in STRIPS:
            across[n].start()

    for pair in order[3:]:
        loaded(*pair)
    for row, col in ((2, 0), (2, 1), (3, 1), (2, 4), (3, 4), (3, 5)):
        at(x, col, row)[...] = at(x, row, col)[...].T

    def square(row, col, first, last):
        value = product(at(x, row, first, 1, last - first)[...], at(x, first, col, last - first, 1)[...])
        at(s, row - 2, col)[...] = (value * keep(row, col)).astype(BF16)

    square(2, 2, 0, 5)

    @when(jnp.logical_or(place == 1, jnp.logical_and(first_in_run, even_run)))
    def _():
        pl.semaphore_wait(ready, 1)

    @when(crossing, first_in_run)
    def _():
        for n in STRIPS:
            across[n].start()

    forward(0)
    square(3, 3, 1, 6)
    forward(1)
    square(2, 3, 1, 5)
    at(s, 1, 2)[...] = at(s, 0, 3)[...].T

    def local(n, c):
        total[:, pl.ds(c, B)] = product(at(s, 0, 2, 2, 2)[...], x[2 * B : 4 * B, pl.ds(c, B)])

    over(1, 3, local)
    forward(2)
    over(3, 5, local)
    at(total, 0, 0)[...] = product(at(s, 0, 2)[...], at(x, 2, 0)[...])
    forward(3)
    at(total, 1, 5)[...] = product(at(s, 1, 3)[...], at(x, 3, 5)[...])
    partial[:, :B] = product(at(x, 2, 2, 2, 2)[...], at(x, 2, 4, 2, 1)[...])
    partial[B:, B:] = product(at(x, 3, 3)[...], at(x, 3, 5)[...])
    forward(4)
    part20, part21, part31 = partial.at[:B, B:], at(total, 0, 5), at(total, 1, 0)
    part20[...] = product(at(x, 2, 2)[...], at(x, 2, 0)[...])
    value = product(at(x, 2, 2, 2, 2)[...], at(x, 2, 1, 2, 1)[...])
    part21[...] = value[:B]
    part31[...] = value[B:]
    left[...] = at(x, 3, 5)[...]
    last_rows[:, :B] = at(x, 5, 3)[...]
    forward(5)

    def finish(row, col, value):
        scale = keep(row, col) * FACTOR
        block = 1.5 * at(x, row, col)[...].astype(F32) - scale * value
        if (row, col) in LATE:
            base[:, (col - 3) * B : (col - 2) * B] = block
        else:
            done[row - 2, col - (row - 2)] = block.astype(BF16)

    def low_01():
        arrived(even, *STRIPS)
        at(x, 0, 1)[...] = sides[low]
        at(x, 1, 0)[...] = sides[low].T
        part20[...] += product(at(x, 2, 1)[...], at(x, 1, 0)[...])
        part21[...] += product(at(x, 2, 0)[...], at(x, 0, 1)[...])

    def low_00():
        arrived(even, 0, 6, 7)
        unpack_side(tiles.at[low, 0], at(x, 0, 0))
        unpack(tiles.at[low, 2], lines.at[low], 0, at(x, 0, 0))
        at(s, 0, 0)[...] = ((part20[...] + product(at(x, 2, 0)[...], at(x, 0, 0)[...])) * keep(2, 0)).astype(BF16)

    def low_11():
        arrived(even, 1, 8)
        unpack_side(tiles.at[low, 1], at(x, 1, 1))
        unpack(tiles.at[low, 3], lines.at[low], 1, at(x, 1, 1))
        at(s, 0, 1)[...] = ((part21[...] + product(at(x, 2, 1)[...], at(x, 1, 1)[...])) * keep(2, 1)).astype(BF16)
        at(s, 1, 1)[...] = ((part31[...] + product(at(x, 3, 1)[...], at(x, 1, 1)[...])) * keep(3, 1)).astype(BF16)
        finish(2, 0, at(total, 0, 0)[...] + product(at(s, 0, 0, 1, 2)[...], at(x, 0, 0, 2, 1)[...]))
        finish(2, 1, at(total, 0, 1)[...] + product(at(s, 0, 0, 1, 2)[...], at(x, 0, 1, 2, 1)[...]))
        at(total, 0, 2)[...] += product(at(s, 0, 0, 1, 2)[...], at(x, 0, 2, 2, 1)[...])
        at(total, 0, 3)[...] += product(at(s, 0, 1)[...], at(x, 1, 3)[...])
        finish(3, 1, at(total, 1, 1)[...] + product(at(s, 1, 1)[...], at(x, 1, 1)[...]))
        for col in (2, 3):
            at(total, 1, col)[...] += product(at(s, 1, 1)[...], at(x, 1, col)[...])

    def high_44():
        arrived(odd, 0, 6, 7)
        unpack_side(tiles.at[high, 0], at(x, 4, 4))
        unpack(tiles.at[high, 2], lines.at[high], 0, at(x, 4, 4))
        value = partial[:, :B] + product(at(x, 2, 4, 2, 1)[...], at(x, 4, 4)[...])
        at(s, 0, 4)[...] = (value[:B] * keep(2, 4)).astype(BF16)
        partial[B:, :B] = value[B:]
        for col in (2, 3):
            at(total, 0, col)[...] += product(at(s, 0, 4)[...], at(x, 4, col)[...])
        finish(2, 4, at(total, 0, 4)[...] + product(at(s, 0, 4)[...], at(x, 4, 4)[...]))

    def high_45():
        arrived(odd, *STRIPS)
        at(x, 4, 5)[...] = sides[high]
        at(x, 5, 4)[...] = sides[high].T
        last_rows[:, B:] = at(x, 5, 4)[...]
        value = partial[B:, :B] + product(at(x, 3, 5)[...], at(x, 5, 4)[...])
        at(s, 1, 4)[...] = (value * keep(3, 4)).astype(BF16)
        for col in (2, 3):
            at(total, 1, col)[...] += product(at(s, 1, 4)[...], at(x, 4, col)[...])
        for col in (4, 5):
            finish(3, col, at(total, 1, col)[...] + product(at(s, 1, 4)[...], at(x, 4, col)[...]))
        arrived(odd, 1)
        side = tiles[high, 1]
        value = partial[B:, B:] + product(at(x, 3, 4)[...], at(x, 4, 5)[...])
        part_square[:, :H] = value[:, :H] + product(left[:, H:], side.T)
        part_square[:, H:] = value[:, H:] + product(left[:, :H], side)
        last_side[...] = side

    pass_on(jnp.logical_not(ends), STRIPS)
    pl.when(odd)(low_01)
    forward(6)
    forward(7)
    pl.when(odd)(low_00)
    pl.when(even)(high_44)
    forward(8)
    pl.when(odd)(low_11)
    pl.when(even)(high_45)
    pass_on(ends, OTHERS)

    @pl.when(odd)
    def _():
        high_44()
        high_45()

    @pl.when(even)
    def _():
        low_01()
        low_00()
        low_11()

    for row, col in ((2, 2), (2, 3), (3, 2), (3, 3)):
        finish(row, col, at(total, row - 2, col)[...])
    arrived(odd, 8)
    last_tile[...] = tiles[high, 3]
    last_diagonals[...] = lines[high]

    for n in range(PIECES):
        direct[n].wait_send()
        when(jnp.logical_not(spared))(onward[n].wait_send)
    for condition, copies, pieces in (
        (spared, aside, OTHERS),
        (crossing, across, STRIPS),
        (jnp.logical_and(relay, ends), relays, OTHERS),
        (jnp.logical_and(relay, jnp.logical_not(ends)), relays, STRIPS),
    ):

        @when(condition)
        def _():
            for n in pieces:
                copies[n].wait_send()


def tail(occupancy, done, base, part_square, left, last_rows, last_side, last_tile, last_diagonals, out, corner, late, store_sem):
    stores = []

    def store(source, row, col):
        place = (row - 2, col - (row - 2))
        copy = pltpu.make_async_copy(source, out.at[place], store_sem.at[place])
        copy.start()
        stores.append(copy)

    for row, col in EARLY:
        store(done.at[row - 2, col - (row - 2)], row, col)
    unpack_side(last_side, corner)
    unpack(last_tile, last_diagonals, 1, corner)
    squares = []
    for half in (slice(0, H), slice(H, B)):
        value = part_square[:, half] + product(left[:, half], corner[half, half])
        squares.append((value * occupancy[1, 4].astype(F32)).astype(BF16))
    square = jnp.concatenate(squares, axis=1)
    rows = [last_rows.at[:, :B], last_rows.at[:, B:], corner]
    for n, (row, col) in enumerate(LATE):
        scale = occupancy[row - 2, col - (row - 2)].astype(F32) * FACTOR
        value = product(square, rows[n][...])
        late[n] = (base[:, n * B : (n + 1) * B] - scale * value).astype(BF16)
        store(late.at[n], row, col)
    for copy in stores:
        copy.wait()


def on_device(band_blocks, occupancy):
    dma = pltpu.SemaphoreType.DMA
    vmem = pl.BlockSpec(memory_space=pltpu.VMEM)
    smem = pl.BlockSpec(memory_space=pltpu.SMEM)
    hbm = pl.BlockSpec(memory_space=pl.ANY)
    held = pl.pallas_call(
        kernel,
        out_shape=(
            pltpu.VMEM(band_blocks.shape, BF16),
            pltpu.VMEM((B, 3 * B), F32),
            pltpu.VMEM((B, B), F32),
            pltpu.VMEM((B, B), BF16),
            pltpu.VMEM((B, 2 * B), BF16),
            pltpu.VMEM((H, H), BF16),
            pltpu.VMEM((H, H), BF16),
            pltpu.VMEM((16, H // 2), BF16),
        ),
        in_specs=[hbm, hbm],
        out_specs=(vmem,) * 8,
        scratch_shapes=[
            pltpu.VMEM((SPAN * B, SPAN * B), BF16),
            pltpu.VMEM((OWN * B, SPAN * B), BF16),
            pltpu.VMEM((OWN * B, SPAN * B), F32),
            pltpu.VMEM((OWN * B, 2 * B), F32),
            pltpu.VMEM((2, H, H), BF16),
            pltpu.VMEM((16, H // 2), BF16),
            pltpu.VMEM((3, 4, H, H), BF16),
            pltpu.VMEM((3, B, B), BF16),
            pltpu.VMEM((3, 16, H // 2), BF16),
            pltpu.SMEM((OWN, SLOTS), jnp.int32),
            dma((OWN * SLOTS + 1,)),
            dma((3, PIECES)),
            dma((3, PIECES)),
            pltpu.SemaphoreType.REGULAR,
        ],
        compiler_params=pltpu.CompilerParams(
            collective_id=0, has_side_effects=True, vmem_limit_bytes=48 * MIB
        ),
        name="step",
    )(band_blocks, occupancy)
    return pl.pallas_call(
        tail,
        out_shape=jax.ShapeDtypeStruct(band_blocks.shape, BF16),
        in_specs=[smem] + [vmem] * 8,
        out_specs=hbm,
        scratch_shapes=[pltpu.VMEM((B, B), BF16), pltpu.VMEM((3, B, B), BF16), dma((OWN, SLOTS))],
        compiler_params=pltpu.CompilerParams(vmem_limit_bytes=12 * MIB),
        name="finish",
    )(occupancy, *held)


def solution(mesh):
    return jax.shard_map(
        on_device,
        mesh=mesh,
        in_specs=(P(("row", "col"), None, None, None), P(("row", "col"), None)),
        out_specs=P(("row", "col"), None, None, None),
        check_vma=False,
    )
```

```python
import functools

import jax
import jax.numpy as jnp
from jax import lax
from jax.experimental import pallas as pl
from jax.experimental.pallas import tpu as pltpu
from jax.sharding import PartitionSpec as P

F32, BF16 = jnp.float32, jnp.bfloat16
MESH = pl.DeviceIdType.MESH
B = 512
H = B // 2
OWN = 2
SLOTS = 5
SPAN = 6
MIB = 2**20
FACTOR = 0.5 / (SLOTS * B)
CORNER = ((2, 2), (2, 3), (3, 3))
PIECES = 9
STRIPS = (2, 3, 4, 5)
OTHERS = (0, 1, 6, 7, 8)
STRIP = B // len(STRIPS)
INSIDE = [(row, col) for row in (2, 3) for col in range(row - 2, row + 3)]
EARLY = [(2, 0), (2, 1), (2, 2), (2, 3), (2, 4), (3, 1), (3, 2)]
LATE = [(3, 3), (3, 4), (3, 5)]


def chain(step):
    rows, cols = lax.axis_size("row"), lax.axis_size("col")
    place = lax.axis_index("row") * cols + lax.axis_index("col")
    other = lax.rem(place + (step + rows * cols), rows * cols)
    return {"row": lax.div(other, cols), "col": lax.rem(other, cols)}


def at(ref, row, col, height=1, width=1):
    return ref.at[row * B : (row + height) * B, col * B : (col + width) * B]


def product(left, right):
    return jnp.dot(left, right, preferred_element_type=F32)


def over(first, last, body):
    def step(n, carry):
        body(n, pl.multiple_of(n * B, B))
        return carry

    lax.fori_loop(first, last, step, 0)


def ramps():
    row = lax.broadcasted_iota(jnp.int32, (H, H), 0)
    col = lax.broadcasted_iota(jnp.int32, (H, H), 1)
    return row, col


def pack(block, tile):
    row, col = ramps()
    first, second = block[:H, :H].astype(F32), block[H:, H:].astype(F32)
    tile[...] = jnp.where(row <= col, first, second).astype(BF16)
    diagonal = jnp.sum(jnp.where(row == col, second, 0.0), axis=0, keepdims=True)
    return [diagonal[:, : H // 2], diagonal[:, H // 2 :]]


def unpack_side(side, block):
    block[:H, H:] = side[...]
    block[H:, :H] = side[...].T


def unpack(tile, diagonals, n, block):
    row, col = ramps()
    tile = tile[...].astype(F32)
    turned = tile.T
    lines = diagonals[...].astype(F32)
    diagonal = jnp.concatenate([lines[2 * n : 2 * n + 1], lines[2 * n + 1 : 2 * n + 2]], axis=1)
    block[:H, :H] = jnp.where(row <= col, tile, turned).astype(BF16)
    block[H:, H:] = jnp.where(row > col, tile, jnp.where(row < col, turned, diagonal)).astype(BF16)


def kernel(
    band, occupied, done, base, part_square, left, last_rows, last_side, last_tile, last_diagonals,
    x, s, total, partial, packed, diagonals, tiles, sides, lines,
    occupancy, load_sem, send_sem, recv_sem, ready,
):
    place, last = lax.axis_index("col"), lax.axis_size("col") - 1
    parity = lax.rem(place, 2)
    even, odd = parity == 0, parity == 1
    first_in_run, last_in_run = place == 0, place == last
    step = 1 - 2 * parity
    partner, target, origin = chain(step), chain(2 * step), chain(-2 * step)
    low, high = 1 - parity, parity
    cols = last + 1
    odd_run = lax.rem(lax.axis_index("row"), 2) == 1
    even_run = jnp.logical_not(odd_run)
    head, foot = place <= 1, place >= last - 1
    far = jnp.logical_or(jnp.logical_and(odd_run, foot), jnp.logical_and(even_run, head))
    relay = jnp.logical_and(jnp.logical_or(head, foot), jnp.logical_not(far))
    ends = jnp.logical_or(first_in_run, last_in_run)
    crossing = jnp.logical_and(far, ends)
    spared = jnp.logical_and(far, jnp.logical_not(ends))
    other_end = chain(jnp.where(head, last - 1, 1 - last))
    beyond = chain(jnp.where(head, cols - place, last - place - cols))

    def signal(semaphore, device):
        pl.semaphore_signal(semaphore, inc=1, device_id=device, device_id_type=MESH)

    def when(condition, *more):
        for other in more:
            condition = jnp.logical_and(condition, other)
        return pl.when(condition)

    barrier = pltpu.get_barrier_semaphore()
    signal(barrier, partner)

    @when(jnp.logical_not(last_in_run), jnp.logical_not(jnp.logical_and(first_in_run, even_run)))
    def _():
        signal(barrier, origin)

    @when(head)
    def _():
        signal(barrier, other_end)

    @when(place == 1, odd_run)
    def _():
        signal(barrier, chain(-2))

    @when(crossing)
    def _():
        for n in (0, 1):
            signal(barrier, chain(jnp.where(last_in_run, cols - n, n - cols)))

    def keep(row, col):
        return occupancy[row - OWN, col - (row - OWN)].astype(F32)

    order = [(2, 3), (2, 2), (3, 3)]
    order += [pair for pair in INSIDE if pair not in order]
    loads = {}
    for n, (row, col) in enumerate(order):
        loads[row, col] = pltpu.make_async_copy(
            band.at[row - 2, col - (row - 2)], at(x, row, col), load_sem.at[n]
        )
        loads[row, col].start()
    flags = pltpu.make_async_copy(occupied, occupancy, load_sem.at[len(order)])
    flags.start()

    def loaded(row, col):
        loads[row, col].wait()
        block = at(x, row, col)
        block[...] = (block[...].astype(F32) * keep(row, col)).astype(BF16)

    def landing(slot, n):
        if n < 2:
            return tiles.at[slot, n]
        if n < 6:
            return sides.at[slot, (n - 2) * STRIP : (n - 1) * STRIP]
        return lines.at[slot] if n == 6 else tiles.at[slot, n - 5]

    def strip(n):
        return x.at[2 * B + (n - 2) * STRIP : 2 * B + (n - 1) * STRIP, 3 * B : 4 * B]

    sources = [band.at[0, 2, :H, H:], band.at[1, 2, :H, H:]] + [strip(n) for n in STRIPS]
    sources += [diagonals, packed.at[0], packed.at[1]]

    def remote(source, slot, kind, n, device):
        return pltpu.make_async_remote_copy(
            src_ref=source,
            dst_ref=landing(slot, n),
            send_sem=send_sem.at[kind, n],
            recv_sem=recv_sem.at[slot, n],
            device_id=device,
            device_id_type=MESH,
        )

    direct = [remote(sources[n], 0, 0, n, partner) for n in range(PIECES)]
    onward = [remote(landing(0, n), 1, 1, n, target) for n in range(PIECES)]
    aside = {n: remote(landing(0, n), 2, 1, n, other_end) for n in OTHERS}
    across = {n: remote(strip(n), 2, 2, n, other_end) for n in STRIPS}
    relays = [remote(landing(2, n), 1, 2, n, beyond) for n in range(PIECES)]

    def forward(n):
        direct[n].wait_recv()
        when(jnp.logical_not(spared))(onward[n].start)
        if n in OTHERS:
            when(spared)(aside[n].start)

    def pass_on(condition, pieces):
        @when(relay, condition)
        def _():
            for n in pieces:
                across[n].wait_recv() if n in STRIPS else aside[n].wait_recv()
                relays[n].start()

    def arrived(relayed, *pieces):
        @when(relayed)
        def _():
            for n in pieces:
                onward[n].wait_recv()

    for run, counts in ((odd_run, (3, 2, 2, 3)), (even_run, (2, 1, 4, 5))):
        for position, count in zip((0, 1, last - 1, last), counts):

            @when(run, place == position)
            def _():
                pl.semaphore_wait(barrier, count)

    @when(jnp.logical_not(jnp.logical_or(head, foot)))
    def _():
        pl.semaphore_wait(barrier, 2)

    @when(even_run, foot)
    def _():
        signal(ready, other_end)

    @when(even_run, last_in_run)
    def _():
        signal(ready, chain(2))

    direct[0].start()
    direct[1].start()
    flags.wait()
    loaded(2, 3)
    for n in STRIPS:
        direct[n].start()
    loaded(2, 2)
    first = pack(at(x, 2, 2), packed.at[0])
    loaded(3, 3)
    second = pack(at(x, 3, 3), packed.at[1])
    diagonals[...] = jnp.concatenate(first + second + [jnp.zeros((12, H // 2), F32)], axis=0).astype(BF16)
    for n in (6, 7, 8):
        direct[n].start()

    @when(crossing, last_in_run)
    def _():
        for n in STRIPS:
            across[n].start()

    for pair in order[3:]:
        loaded(*pair)
    for row, col in ((2, 0), (2, 1), (3, 1), (2, 4), (3, 4), (3, 5)):
        at(x, col, row)[...] = at(x, row, col)[...].T

    def square(row, col, first, last):
        value = product(at(x, row, first, 1, last - first)[...], at(x, first, col, last - first, 1)[...])
        at(s, row - 2, col)[...] = (value * keep(row, col)).astype(BF16)

    square(2, 2, 0, 5)

    @when(jnp.logical_or(place == 1, jnp.logical_and(first_in_run, even_run)))
    def _():
        pl.semaphore_wait(ready, 1)

    @when(crossing, first_in_run)
    def _():
        for n in STRIPS:
            across[n].start()

    forward(0)
    square(3, 3, 1, 6)
    forward(1)
    square(2, 3, 1, 5)
    at(s, 1, 2)[...] = at(s, 0, 3)[...].T

    def local(n, c):
        total[:, pl.ds(c, B)] = product(at(s, 0, 2, 2, 2)[...], x[2 * B : 4 * B, pl.ds(c, B)])

    over(1, 3, local)
    forward(2)
    over(3, 5, local)
    at(total, 0, 0)[...] = product(at(s, 0, 2)[...], at(x, 2, 0)[...])
    forward(3)
    at(total, 1, 5)[...] = product(at(s, 1, 3)[...], at(x, 3, 5)[...])
    partial[:, :B] = product(at(x, 2, 2, 2, 2)[...], at(x, 2, 4, 2, 1)[...])
    partial[B:, B:] = product(at(x, 3, 3)[...], at(x, 3, 5)[...])
    forward(4)
    part20, part21, part31 = partial.at[:B, B:], at(total, 0, 5), at(total, 1, 0)
    part20[...] = product(at(x, 2, 2)[...], at(x, 2, 0)[...])
    value = product(at(x, 2, 2, 2, 2)[...], at(x, 2, 1, 2, 1)[...])
    part21[...] = value[:B]
    part31[...] = value[B:]
    left[...] = at(x, 3, 5)[...]
    last_rows[:, :B] = at(x, 5, 3)[...]
    forward(5)

    def finish(row, col, value):
        scale = keep(row, col) * FACTOR
        block = 1.5 * at(x, row, col)[...].astype(F32) - scale * value
        if (row, col) in LATE:
            base[:, (col - 3) * B : (col - 2) * B] = block
        else:
            done[row - 2, col - (row - 2)] = block.astype(BF16)

    def gather(last_part, row, col, value):
        value = at(total, row - 2, col)[...] + value
        if last_part:
            finish(row, col, value)
        else:
            at(total, row - 2, col)[...] = value

    def low_01():
        arrived(even, *STRIPS)
        at(x, 0, 1)[...] = sides[low]
        at(x, 1, 0)[...] = sides[low].T
        part20[...] += product(at(x, 2, 1)[...], at(x, 1, 0)[...])
        part21[...] += product(at(x, 2, 0)[...], at(x, 0, 1)[...])

    def low_00():
        arrived(even, 0, 6, 7)
        unpack_side(tiles.at[low, 0], at(x, 0, 0))
        unpack(tiles.at[low, 2], lines.at[low], 0, at(x, 0, 0))
        at(s, 0, 0)[...] = ((part20[...] + product(at(x, 2, 0)[...], at(x, 0, 0)[...])) * keep(2, 0)).astype(BF16)

    def low_11(last_part):
        arrived(even, 1, 8)
        unpack_side(tiles.at[low, 1], at(x, 1, 1))
        unpack(tiles.at[low, 3], lines.at[low], 1, at(x, 1, 1))
        at(s, 0, 1)[...] = ((part21[...] + product(at(x, 2, 1)[...], at(x, 1, 1)[...])) * keep(2, 1)).astype(BF16)
        at(s, 1, 1)[...] = ((part31[...] + product(at(x, 3, 1)[...], at(x, 1, 1)[...])) * keep(3, 1)).astype(BF16)
        finish(2, 0, at(total, 0, 0)[...] + product(at(s, 0, 0, 1, 2)[...], at(x, 0, 0, 2, 1)[...]))
        finish(2, 1, at(total, 0, 1)[...] + product(at(s, 0, 0, 1, 2)[...], at(x, 0, 1, 2, 1)[...]))
        gather(last_part, 2, 2, product(at(s, 0, 0, 1, 2)[...], at(x, 0, 2, 2, 1)[...]))
        gather(last_part, 2, 3, product(at(s, 0, 1)[...], at(x, 1, 3)[...]))
        finish(3, 1, at(total, 1, 1)[...] + product(at(s, 1, 1)[...], at(x, 1, 1)[...]))
        for col in (2, 3):
            gather(last_part, 3, col, product(at(s, 1, 1)[...], at(x, 1, col)[...]))

    def high_44(last_part):
        arrived(odd, 0, 6, 7)
        unpack_side(tiles.at[high, 0], at(x, 4, 4))
        unpack(tiles.at[high, 2], lines.at[high], 0, at(x, 4, 4))
        value = partial[:, :B] + product(at(x, 2, 4, 2, 1)[...], at(x, 4, 4)[...])
        at(s, 0, 4)[...] = (value[:B] * keep(2, 4)).astype(BF16)
        partial[B:, :B] = value[B:]
        for col in (2, 3):
            gather(last_part, 2, col, product(at(s, 0, 4)[...], at(x, 4, col)[...]))
        finish(2, 4, at(total, 0, 4)[...] + product(at(s, 0, 4)[...], at(x, 4, 4)[...]))

    def high_45(last_part):
        arrived(odd, *STRIPS)
        at(x, 4, 5)[...] = sides[high]
        at(x, 5, 4)[...] = sides[high].T
        last_rows[:, B:] = at(x, 5, 4)[...]
        value = partial[B:, :B] + product(at(x, 3, 5)[...], at(x, 5, 4)[...])
        at(s, 1, 4)[...] = (value * keep(3, 4)).astype(BF16)
        for col in (2, 3):
            gather(last_part, 3, col, product(at(s, 1, 4)[...], at(x, 4, col)[...]))
        for col in (4, 5):
            finish(3, col, at(total, 1, col)[...] + product(at(s, 1, 4)[...], at(x, 4, col)[...]))
        arrived(odd, 1)
        side = tiles[high, 1]
        value = partial[B:, B:] + product(at(x, 3, 4)[...], at(x, 4, 5)[...])
        part_square[:, :H] = value[:, :H] + product(left[:, H:], side.T)
        part_square[:, H:] = value[:, H:] + product(left[:, :H], side)
        last_side[...] = side

    pass_on(jnp.logical_not(ends), STRIPS)
    pass_on(ends, OTHERS[:2])
    pl.when(odd)(low_01)
    forward(6)
    forward(7)
    pl.when(odd)(low_00)
    pl.when(even)(functools.partial(high_44, False))
    forward(8)
    pass_on(last_in_run, OTHERS[2:])
    pl.when(odd)(functools.partial(low_11, False))
    pl.when(even)(functools.partial(high_45, False))
    pass_on(first_in_run, OTHERS[2:])

    @pl.when(odd)
    def _():
        high_44(True)
        high_45(True)

    @pl.when(even)
    def _():
        low_01()
        low_00()
        low_11(True)

    arrived(odd, 8)
    last_tile[...] = tiles[high, 3]
    last_diagonals[...] = lines[high]

    for n in range(PIECES):
        direct[n].wait_send()
        when(jnp.logical_not(spared))(onward[n].wait_send)
    for condition, copies, pieces in (
        (spared, aside, OTHERS),
        (crossing, across, STRIPS),
        (jnp.logical_and(relay, ends), relays, OTHERS),
        (jnp.logical_and(relay, jnp.logical_not(ends)), relays, STRIPS),
    ):

        @when(condition)
        def _():
            for n in pieces:
                copies[n].wait_send()


def tail(occupancy, done, base, part_square, left, last_rows, last_side, last_tile, last_diagonals, out, corner, late, store_sem):
    stores = []

    def store(source, row, col):
        place = (row - 2, col - (row - 2))
        copy = pltpu.make_async_copy(source, out.at[place], store_sem.at[place])
        copy.start()
        stores.append(copy)

    for row, col in EARLY:
        store(done.at[row - 2, col - (row - 2)], row, col)
    unpack_side(last_side, corner)
    unpack(last_tile, last_diagonals, 1, corner)
    squares = []
    for half in (slice(0, H), slice(H, B)):
        value = part_square[:, half] + product(left[:, half], corner[half, half])
        squares.append((value * occupancy[1, 4].astype(F32)).astype(BF16))
    square = jnp.concatenate(squares, axis=1)
    rows = [last_rows.at[:, :B], last_rows.at[:, B:], corner]
    for n, (row, col) in enumerate(LATE):
        scale = occupancy[row - 2, col - (row - 2)].astype(F32) * FACTOR
        value = product(square, rows[n][...])
        late[n] = (base[:, n * B : (n + 1) * B] - scale * value).astype(BF16)
        store(late.at[n], row, col)
    for copy in stores:
        copy.wait()


def on_device(band_blocks, occupancy):
    dma = pltpu.SemaphoreType.DMA
    vmem = pl.BlockSpec(memory_space=pltpu.VMEM)
    smem = pl.BlockSpec(memory_space=pltpu.SMEM)
    hbm = pl.BlockSpec(memory_space=pl.ANY)
    held = pl.pallas_call(
        kernel,
        out_shape=(
            pltpu.VMEM(band_blocks.shape, BF16),
            pltpu.VMEM((B, 3 * B), F32),
            pltpu.VMEM((B, B), F32),
            pltpu.VMEM((B, B), BF16),
            pltpu.VMEM((B, 2 * B), BF16),
            pltpu.VMEM((H, H), BF16),
            pltpu.VMEM((H, H), BF16),
            pltpu.VMEM((16, H // 2), BF16),
        ),
        in_specs=[hbm, hbm],
        out_specs=(vmem,) * 8,
        scratch_shapes=[
            pltpu.VMEM((SPAN * B, SPAN * B), BF16),
            pltpu.VMEM((OWN * B, SPAN * B), BF16),
            pltpu.VMEM((OWN * B, SPAN * B), F32),
            pltpu.VMEM((OWN * B, 2 * B), F32),
            pltpu.VMEM((2, H, H), BF16),
            pltpu.VMEM((16, H // 2), BF16),
            pltpu.VMEM((3, 4, H, H), BF16),
            pltpu.VMEM((3, B, B), BF16),
            pltpu.VMEM((3, 16, H // 2), BF16),
            pltpu.SMEM((OWN, SLOTS), jnp.int32),
            dma((OWN * SLOTS + 1,)),
            dma((3, PIECES)),
            dma((3, PIECES)),
            pltpu.SemaphoreType.REGULAR,
        ],
        compiler_params=pltpu.CompilerParams(
            collective_id=0, has_side_effects=True, vmem_limit_bytes=48 * MIB
        ),
        name="step",
    )(band_blocks, occupancy)
    return pl.pallas_call(
        tail,
        out_shape=jax.ShapeDtypeStruct(band_blocks.shape, BF16),
        in_specs=[smem] + [vmem] * 8,
        out_specs=hbm,
        scratch_shapes=[pltpu.VMEM((B, B), BF16), pltpu.VMEM((3, B, B), BF16), dma((OWN, SLOTS))],
        compiler_params=pltpu.CompilerParams(vmem_limit_bytes=12 * MIB),
        name="finish",
    )(occupancy, *held)


def solution(mesh):
    return jax.shard_map(
        on_device,
        mesh=mesh,
        in_specs=(P(("row", "col"), None, None, None), P(("row", "col"), None)),
        out_specs=P(("row", "col"), None, None, None),
        check_vma=False,
    )
```
